32 devices in a mesh: groups: 2 (over y), cols: 4 (over z), tok: 2 (over x), sub: 2 (over core).
Axes of the slice: x: 2, y: 2, z: 4, core: 2. Of those that a mesh axis runs over, the one named last changes fastest.
Arguments:
- tokens: bfloat16 [2048, 8192], P(('groups', 'tok'), 'cols'), parts along dimension 0
- damp_ratio: int32 [2], P('groups'), parts along dimension 0, may hold values from 1 to 10, as said below
- panel_index: int32 [2], P('groups'), parts along dimension 0, may hold values from 0 to 14
Outputs:
- updated: float32 [16384, 8192], P(('groups', 'tok', 'sub'), 'cols'), parts along dimension 0
- panel: float32 [16384, 512], P(('groups', 'tok', 'sub')), parts along dimension 0
The draws below stay inside these ranges and needn't reach their ends.
There are 2 independent parts, one for each index of `groups`. The reference program is written for one: setup_inputs(seed, part) draws one part's arguments, and reference() takes and returns one part's arrays. A program takes and returns all parts, laid end to end along the dimension named above; each array names one. Nothing has to cross between parts.
Inputs may be any that keep to these rules, and one draw needn't show every extreme that they name: `damp_ratio`: every odd-numbered part has the most. `panel_index`: a trailing block always follows the panel.
All inputs are finite; a program needn't handle non-finite values.
Results may differ from the reference program's by a relative error of at most 0.0003.
Values may be sent and summed in bfloat16 or wider, within the bound.
A program may use at most 192 MiB of HBM per device.

```python
import jax
import jax.numpy as jnp
from jax import lax

D = 8192
PANEL = 512
TOKENS = 1024


def draw_tokens(key, part):
    key = jax.random.fold_in(key, 11)
    scale_key, entry_key = jax.random.split(key, 2)
    ramp = jnp.arange(D, dtype=jnp.float32) / D
    col_scale = 0.4 * jnp.power(3.0, ramp) * jnp.exp(jax.random.uniform(scale_key, (D,), jnp.float32, -0.7, 0.7))
    entries = jnp.clip(jax.random.normal(entry_key, (TOKENS, D), jnp.float32), -5.0, 5.0)
    return (entries * col_scale[None, :]).astype(jnp.bfloat16)


def draw_damp_ratio(key, part):
    key = jax.random.fold_in(key, 23)
    lower_value = jax.random.randint(key, (1,), 1, 10, dtype=jnp.int32)
    parity = jnp.asarray(part, jnp.int32) % 2
    return jnp.where(parity == 1, jnp.full((1,), 10, jnp.int32), lower_value).astype(jnp.int32)


def setup_inputs(seed: int = 0, part: int = 0) -> dict:
    seeds = jax.random.split(jax.random.key(seed), 4)
    own_keys = jax.random.split(jax.random.fold_in(seeds[3], part), 4)
    return {
        "tokens": draw_tokens(jax.random.fold_in(jax.random.fold_in(seeds[3], part), 71), part),
        "damp_ratio": draw_damp_ratio(jax.random.fold_in(jax.random.fold_in(seeds[3], part), 71), part),
        "panel_index": jax.random.randint(own_keys[2], (1,), 0, D // PANEL - 1).astype(jnp.int32),
    }


def reference(tokens, damp_ratio, panel_index):
    gram_sum = lax.dot_general(tokens.astype(jnp.float32), tokens.astype(jnp.float32), (((0,), (0,)), ((), ())), preferred_element_type=jnp.float32) * (2.0 / TOKENS)
    diag_mean = jnp.mean(jnp.diagonal(gram_sum))
    damping = damp_ratio[0].astype(jnp.float32) / 100.0 * diag_mean
    hessian = gram_sum + damping * jnp.eye(D, dtype=jnp.float32)
    panel_start = panel_index[0].astype(jnp.int32) * PANEL
    columns = lax.dynamic_slice_in_dim(hessian, panel_start, PANEL, 1)
    diagonal_block = lax.dynamic_slice_in_dim(columns, panel_start, PANEL, 0)
    factor = jnp.linalg.cholesky(diagonal_block)
    solved = jax.scipy.linalg.solve_triangular(factor, columns.T, lower=True).T
    positions = jnp.arange(D, dtype=jnp.int32)
    panel = jnp.where(positions[:, None] >= panel_start, solved, 0.0)
    trailing = positions >= panel_start + PANEL
    update = jnp.dot(panel, panel.T, precision=lax.Precision.HIGHEST)
    updated = hessian - jnp.where(trailing[:, None] & trailing[None, :], update, 0.0)
    return (updated, panel)
```

```python
import jax
import jax.numpy as jnp
from jax import lax
from jax.experimental import pallas as pl
from jax.experimental.pallas import tpu as pltpu
from jax.sharding import PartitionSpec as P

D = 8192
PANEL = 512
BLOCK = 128
GROUP = 4


def exact_dot(a, b, contract):
    return lax.dot_general(
        a, b, (contract, ((), ())), precision=lax.Precision.HIGHEST, preferred_element_type=jnp.float32
    )


def eliminate(a):
    n = a.shape[0]
    row = lax.broadcasted_iota(jnp.int32, (n, n), 0)
    col = lax.broadcasted_iota(jnp.int32, (n, n), 1)
    left, right = a, jnp.where(row == col, 1.0, 0.0).astype(jnp.float32)
    top = 0
    upper, inverse = [], []
    for start in range(0, n, GROUP):
        columns = [
            jnp.broadcast_to(left[:, start + j : start + j + 1], left.shape) for j in range(GROUP)
        ]
        rows = top + lax.broadcasted_iota(jnp.int32, left.shape, 0)
        for j in range(GROUP):
            k = start + j
            at = k - top
            scale = lax.rsqrt(columns[j][at : at + 1, :])
            upper.append(left[at : at + 1, :] * scale)
            inverse.append(right[at : at + 1, :] * scale)
            if k == n - 1:
                break
            multiplier = jnp.where(rows > k, columns[j] * scale, 0.0)
            for later in range(j + 1, GROUP):
                columns[later] = columns[later] - multiplier * (columns[later][at : at + 1, :] * scale)
            left = left - multiplier * upper[-1]
            right = right - multiplier * inverse[-1]
        if (start + GROUP) % 8 == 0 and start + GROUP < n:
            done = start + GROUP - top
            left, right, top = left[done:, :], right[done:, :], start + GROUP
    return jnp.concatenate(upper, 0), jnp.concatenate(inverse, 0)


def factor_kernel(block_ref, factor_ref, inverse_ref, rest_ref):
    n = block_ref.shape[0]
    b = BLOCK
    rest_ref[...] = block_ref[...]
    factor_ref[...] = jnp.zeros_like(factor_ref)
    inverse_ref[...] = jnp.zeros_like(inverse_ref)
    row = lax.broadcasted_iota(jnp.int32, (b, b), 0)
    col = lax.broadcasted_iota(jnp.int32, (b, b), 1)
    for o in range(0, n, b):
        e = o + b
        upper, inverse = eliminate(rest_ref[o:e, o:e])
        factor_ref[o:e, o:e] = jnp.where(row <= col, upper, 0.0).T
        inverse_ref[o:e, o:e] = inverse
        if e < n:
            below = exact_dot(rest_ref[e:, o:e], inverse, ((1,), (1,)))
            factor_ref[e:, o:e] = below
            rest_ref[e:, e:] = rest_ref[e:, e:] - exact_dot(below, below, ((1,), (1,)))
        if o:
            crossed = exact_dot(factor_ref[o:e, :o], inverse_ref[:o, :o], ((1,), (0,)))
            inverse_ref[o:e, :o] = -exact_dot(inverse, crossed, ((1,), (0,)))


def factor_and_inverse(block):
    shape = jax.ShapeDtypeStruct(block.shape, jnp.float32)
    return pl.pallas_call(
        factor_kernel,
        out_shape=[shape, shape],
        in_specs=[pl.BlockSpec(memory_space=pltpu.VMEM)],
        out_specs=[pl.BlockSpec(memory_space=pltpu.VMEM)] * 2,
        scratch_shapes=[pltpu.VMEM(block.shape, jnp.float32)],
        compiler_params=pltpu.CompilerParams(vmem_limit_bytes=32 << 20),
        cost_estimate=pl.CostEstimate(flops=10**9, bytes_accessed=4 << 20, transcendentals=0),
        name="factor",
    )(block)


def split_bf16(x, count):
    parts = []
    for _ in range(count):
        high = lax.reduce_precision(x, 8, 7)
        parts.append(high.astype(jnp.bfloat16))
        x = x - high
    return parts


def dot_bf16(a, b, contract):
    return lax.dot_general(a, b, (contract, ((), ())), preferred_element_type=jnp.float32)


def gather_tokens(tokens):
    half = tokens.shape[0] // lax.axis_size("sub")
    mine = lax.dynamic_slice_in_dim(tokens, lax.axis_index("sub") * half, half, 0)
    pieces = lax.all_gather(mine, ("cols", "tok", "sub"))
    return pieces.reshape(lax.axis_size("cols"), -1, tokens.shape[1])


def body(tokens, damp_ratio, panel_index):
    col_width = tokens.shape[1]
    row_count = D // (lax.axis_size("tok") * lax.axis_size("sub"))
    total = tokens.shape[0] * lax.axis_size("tok")
    scale = 2.0 / total
    row_rank = lax.axis_index(("tok", "sub"))
    col_rank = lax.axis_index("cols")
    row_index = row_rank * row_count + jnp.arange(row_count, dtype=jnp.int32)
    col_index = col_rank * col_width + jnp.arange(col_width, dtype=jnp.int32)

    squares = jnp.sum(jnp.square(tokens.astype(jnp.float32)))
    trace = lax.psum(squares, ("cols", "tok")) * scale
    damping = damp_ratio[0].astype(jnp.float32) / 100.0 * (trace / D)

    blocks = gather_tokens(tokens)
    start = panel_index[0] * PANEL
    end = start + PANEL

    def columns(first, width):
        if width <= col_width:
            block = lax.dynamic_index_in_dim(blocks, first // col_width, 0, keepdims=False)
            if width == col_width:
                return block
            return lax.dynamic_slice_in_dim(block, first % col_width, width, 1)
        several = lax.dynamic_slice_in_dim(blocks, first // col_width, width // col_width, 0)
        return jnp.swapaxes(several, 0, 1).reshape(total, width)

    own_rows = columns(row_rank * row_count, row_count)
    own_cols = columns(col_rank * col_width, col_width)
    in_panel = columns(start, PANEL)

    square = dot_bf16(in_panel, in_panel, ((0,), (0,))) * scale
    square = square + damping * jnp.eye(PANEL, dtype=jnp.float32)
    factor, inverse = factor_and_inverse(square)

    lead = sum(dot_bf16(part, in_panel, ((1,), (1,))) for part in split_bf16(inverse, 3)) * scale
    lead_high, lead_low = split_bf16(lead, 2)

    def solved(x):
        return dot_bf16(lead_high, x, ((1,), (0,))) + dot_bf16(lead_low, x, ((1,), (0,)))

    rows_solved = solved(own_rows)
    cols_solved = solved(own_cols)
    panel_out = jnp.where(row_index[:, None] >= end, rows_solved.T, 0.0)
    offset = start - row_rank * row_count
    holds = (offset >= 0) & (offset < row_count)
    offset = jnp.clip(offset, 0, row_count - PANEL)
    kept = lax.dynamic_slice_in_dim(panel_out, offset, PANEL, 0)
    panel_out = lax.dynamic_update_slice_in_dim(panel_out, jnp.where(holds, factor, kept), offset, 0)

    row_high, row_low = split_bf16(jnp.where(row_index[None, :] >= end, rows_solved, 0.0), 2)
    col_high, col_low = split_bf16(jnp.where(col_index[None, :] >= end, cols_solved * (-1.0 / scale), 0.0), 2)
    left = jnp.concatenate([own_rows, row_high, row_high, row_low], 0)
    right = jnp.concatenate([own_cols, col_high, col_low, col_high], 0)
    updated = dot_bf16(left, right, ((0,), (0,))) * scale
    updated = updated + jnp.where(row_index[:, None] == col_index[None, :], damping, 0.0)
    return (updated, panel_out)


def solution(mesh):
    placed = (P(("groups", "tok"), "cols"), P("groups"), P("groups"))
    return jax.shard_map(
        body,
        mesh=mesh,
        in_specs=placed,
        out_specs=(P(("groups", "tok", "sub"), "cols"), P(("groups", "tok", "sub"), None)),
        check_vma=False,
    )
```

```python
import jax
import jax.numpy as jnp
from jax import lax
from jax.experimental import pallas as pl
from jax.experimental.pallas import tpu as pltpu
from jax.sharding import PartitionSpec as P

D = 8192
PANEL = 512
BLOCK = 128
GROUP = 4


def exact_dot(a, b, contract):
    return lax.dot_general(
        a, b, (contract, ((), ())), precision=lax.Precision.HIGHEST, preferred_element_type=jnp.float32
    )


def eliminate(a):
    n = a.shape[0]
    row = lax.broadcasted_iota(jnp.int32, (n, n), 0)
    col = lax.broadcasted_iota(jnp.int32, (n, n), 1)
    left, right = a, jnp.where(row == col, 1.0, 0.0).astype(jnp.float32)
    top = 0
    upper, inverse = [], []
    for start in range(0, n, GROUP):
        columns = [
            jnp.broadcast_to(left[:, start + j : start + j + 1], left.shape) for j in range(GROUP)
        ]
        rows = top + lax.broadcasted_iota(jnp.int32, left.shape, 0)
        for j in range(GROUP):
            k = start + j
            at = k - top
            scale = lax.rsqrt(columns[j][at : at + 1, :])
            upper.append(left[at : at + 1, :] * scale)
            inverse.append(right[at : at + 1, :] * scale)
            if k == n - 1:
                break
            multiplier = jnp.where(rows > k, columns[j] * scale, 0.0)
            for later in range(j + 1, GROUP):
                columns[later] = columns[later] - multiplier * (columns[later][at : at + 1, :] * scale)
            left = left - multiplier * upper[-1]
            right = right - multiplier * inverse[-1]
        if (start + GROUP) % 8 == 0 and start + GROUP < n:
            done = start + GROUP - top
            left, right, top = left[done:, :], right[done:, :], start + GROUP
    return jnp.concatenate(upper, 0), jnp.concatenate(inverse, 0)


def factor_kernel(block_ref, factor_ref, inverse_ref, rest_ref):
    n = block_ref.shape[0]
    b = BLOCK
    rest_ref[...] = block_ref[...]
    factor_ref[...] = jnp.zeros_like(factor_ref)
    inverse_ref[...] = jnp.zeros_like(inverse_ref)
    row = lax.broadcasted_iota(jnp.int32, (b, b), 0)
    col = lax.broadcasted_iota(jnp.int32, (b, b), 1)
    for o in range(0, n, b):
        e = o + b
        upper, inverse = eliminate(rest_ref[o:e, o:e])
        factor_ref[o:e, o:e] = jnp.where(row <= col, upper, 0.0).T
        inverse_ref[o:e, o:e] = inverse
        if e < n:
            below = exact_dot(rest_ref[e:, o:e], inverse, ((1,), (1,)))
            factor_ref[e:, o:e] = below
            rest_ref[e:, e:] = rest_ref[e:, e:] - exact_dot(below, below, ((1,), (1,)))
        if o:
            crossed = exact_dot(factor_ref[o:e, :o], inverse_ref[:o, :o], ((1,), (0,)))
            inverse_ref[o:e, :o] = -exact_dot(inverse, crossed, ((1,), (0,)))


def factor_and_inverse(block):
    shape = jax.ShapeDtypeStruct(block.shape, jnp.float32)
    return pl.pallas_call(
        factor_kernel,
        out_shape=[shape, shape],
        in_specs=[pl.BlockSpec(memory_space=pltpu.VMEM)],
        out_specs=[pl.BlockSpec(memory_space=pltpu.VMEM)] * 2,
        scratch_shapes=[pltpu.VMEM(block.shape, jnp.float32)],
        compiler_params=pltpu.CompilerParams(vmem_limit_bytes=32 << 20),
        cost_estimate=pl.CostEstimate(flops=10**9, bytes_accessed=4 << 20, transcendentals=0),
        name="factor",
    )(block)


def split_bf16(x, count):
    parts = []
    for _ in range(count):
        high = lax.reduce_precision(x, 8, 7)
        parts.append(high.astype(jnp.bfloat16))
        x = x - high
    return parts


def dot_bf16(a, b, contract):
    return lax.dot_general(a, b, (contract, ((), ())), preferred_element_type=jnp.float32)


def gather_kernel(
    index_ref, tokens_ref, rows_ref, cols_ref, panel_ref, squares_ref,
    line, panel_own, squares_own,
    line_send, line_recv, row_send, row_recv, col_send, col_recv,
    share_send, share_recv, small_send, small_recv, local_sem, keep_sem,
):
    z_count, depth, width = line.shape
    chunks = line_recv.shape[1]
    tok_count, sub_count = cols_ref.shape[:2]
    span = rows_ref.shape[0]
    step = depth // chunks
    z, t, s = lax.axis_index("cols"), lax.axis_index("tok"), lax.axis_index("sub")
    rank = t * sub_count + s
    mesh_id = pl.DeviceIdType.MESH

    def peer(zz, tt, ss):
        return {"cols": zz, "tok": tt, "sub": ss}

    def remote(src, dst, send, recv, zz, tt, ss):
        return pltpu.make_async_remote_copy(
            src_ref=src, dst_ref=dst, send_sem=send, recv_sem=recv,
            device_id=peer(zz, tt, ss), device_id_type=mesh_id,
        )

    others = [(dt, ds) for dt in range(tok_count) for ds in range(sub_count) if dt or ds]

    def other(dt, ds):
        return lax.rem(t + dt, tok_count), lax.rem(s + ds, sub_count)

    barrier = pltpu.get_barrier_semaphore()
    for dt, ds in others:
        tt, ss = other(dt, ds)
        pl.semaphore_signal(barrier, inc=1, device_id=peer(z, tt, ss), device_id_type=mesh_id)

    @pl.when(z > 0)
    def _():
        pl.semaphore_signal(barrier, inc=1, device_id=peer(z - 1, t, s), device_id_type=mesh_id)

    @pl.when(z < z_count - 1)
    def _():
        pl.semaphore_signal(barrier, inc=1, device_id=peer(z + 1, t, s), device_id_type=mesh_id)

    fetch = pltpu.make_async_copy(tokens_ref.at[pl.ds(s * depth, depth)], line.at[z], local_sem.at[0])
    fetch.start()
    sides = jnp.where(z > 0, 1, 0) + jnp.where(z < z_count - 1, 1, 0)
    pl.semaphore_wait(barrier, len(others) + sides)
    fetch.wait()

    def hop(b, q, up):
        part = line.at[b, pl.ds(q * step, step)]
        return remote(
            part, part, line_send.at[up, b, q], line_recv.at[b, q], z + (1 if up else -1), t, s
        )

    def row_copy(b, q, tt, ss):
        return remote(
            line.at[b, pl.ds(q * step, step)],
            rows_ref.at[lax.rem(b, span), t, s, pl.ds(q * step, step)],
            row_send.at[b, q], row_recv.at[lax.rem(b, span), t, s, q], z, tt, ss,
        )

    def row_keep(b, q):
        return pltpu.make_async_copy(
            line.at[b, pl.ds(q * step, step)],
            rows_ref.at[lax.rem(b, span), t, s, pl.ds(q * step, step)],
            keep_sem.at[lax.rem(b, span), q],
        )

    def to_owner(b, q, act):
        owner = b // span

        @pl.when(owner == rank)
        def _():
            act(row_keep(b, q))

        @pl.when(owner != rank)
        def _():
            act(row_copy(b, q, owner // sub_count, lax.rem(owner, sub_count)))

    def start_hop(b, q, up, allowed):
        @pl.when(allowed)
        def _():
            hop(b, q, up).start()

    start = index_ref[0] * PANEL
    lanes, tile = 128, 16
    panel_own[...] = jnp.zeros_like(panel_own)
    squares_own[...] = jnp.zeros_like(squares_own)

    def read_block(b):
        if width >= PANEL:
            pairs = [(j * PANEL, 0, PANEL) for j in range(width // PANEL)]
        else:
            pairs = [(0, j * width, width) for j in range(PANEL // width)]
        weights = [
            jnp.where(b * width + source == start + target, 1.0, 0.0).astype(jnp.float32)
            for source, target, _ in pairs
        ]

        def some_rows(i, c):
            r = pl.ds(pl.multiple_of(i * tile, tile), tile)
            x = line[b, r, :].astype(jnp.float32)
            square = x * x
            squares_own[...] += sum(square[:, k : k + lanes] for k in range(0, width, lanes))
            for weight, (source, target, size) in zip(weights, pairs):
                place = (r, slice(target, target + size))
                found = panel_own[place].astype(jnp.float32) + weight * x[:, source : source + size]
                panel_own[place] = found.astype(jnp.bfloat16)
            return c

        lax.fori_loop(0, depth // tile, some_rows, 0)

    def own_chunk(q, c):
        start_hop(z, q, 1, z < z_count - 1)
        start_hop(z, q, 0, z > 0)
        return c

    lax.fori_loop(0, chunks, own_chunk, 0)

    keep_col = pltpu.make_async_copy(line.at[z], cols_ref.at[t, s], local_sem.at[1])
    keep_col.start()

    def col_copy(dt, ds):
        tt, ss = other(dt, ds)
        return remote(
            line.at[z], cols_ref.at[t, s], col_send.at[dt, ds], col_recv.at[t, s], z, tt, ss
        )

    def col_pass(dt, ds):
        tt = lax.rem(t + dt, tok_count)
        ss = lax.rem(s + ds, sub_count)
        return remote(
            cols_ref.at[tt, s], cols_ref.at[tt, s], col_send.at[dt, ds], col_recv.at[tt, s], z, t, ss
        )

    for dt in range(1, tok_count):
        col_copy(dt, 0).start()
    for ds in range(1, sub_count):
        col_copy(0, ds).start()

    def own_rows(q, c):
        to_owner(z, q, lambda copy: copy.start())
        return c

    lax.fori_loop(0, chunks, own_rows, 0)
    read_block(z)

    def arrived(b, q, up, onward):
        hop(b, q, 0).wait_recv()
        start_hop(b, q, up, onward)
        to_owner(b, q, lambda copy: copy.start())

        @pl.when(q == chunks - 1)
        def _():
            read_block(b)

    def travel(i, c):
        d, q = 1 + i // chunks, lax.rem(i, chunks)

        @pl.when(z - d >= 0)
        def _():
            arrived(z - d, q, 1, z < z_count - 1)

        @pl.when(z + d < z_count)
        def _():
            arrived(z + d, q, 0, z > 0)

        return c

    lax.fori_loop(0, (z_count - 1) * chunks, travel, 0)

    def share(dt, ds):
        tt, ss = other(dt, ds)
        return remote(
            panel_own, panel_ref.at[t, s], share_send.at[dt, ds], share_recv.at[t, s], z, tt, ss
        )

    def small(dt, ds):
        tt, ss = other(dt, ds)
        return remote(
            squares_own, squares_ref.at[t, s], small_send.at[dt, ds], small_recv.at[t, s], z, tt, ss
        )

    for dt, ds in others:
        share(dt, ds).start()
    keep_panel = pltpu.make_async_copy(panel_own, panel_ref.at[t, s], local_sem.at[2])
    keep_panel.start()

    for dt in range(1, tok_count):
        tt = lax.rem(t + dt, tok_count)
        remote(line.at[z], cols_ref.at[tt, s], col_send.at[dt, 0], col_recv.at[tt, s], z, tt, s).wait_recv()
        for ds in range(1, sub_count):
            col_pass(dt, ds).start()

    for dt, ds in others:
        small(dt, ds).start()
    keep_squares = pltpu.make_async_copy(squares_own, squares_ref.at[t, s], local_sem.at[3])
    keep_squares.start()

    for dt, ds in others:
        tt, ss = other(dt, ds)
        remote(panel_own, panel_ref.at[tt, ss], share_send.at[dt, ds], share_recv.at[tt, ss], z, tt, ss).wait()
        remote(squares_own, squares_ref.at[tt, ss], small_send.at[dt, ds], small_recv.at[tt, ss], z, tt, ss).wait()
        pair = remote(line.at[z], cols_ref.at[tt, ss], col_send.at[dt, ds], col_recv.at[tt, ss], z, tt, ss)
        pair.wait_send()
        if ds:
            pair.wait_recv()

        def rows_in(i, c, tt=tt, ss=ss):
            b, q = rank * span + i // chunks, lax.rem(i, chunks)
            remote(
                line.at[0, pl.ds(q * step, step)],
                rows_ref.at[i // chunks, tt, ss, pl.ds(q * step, step)],
                row_send.at[b, q], row_recv.at[i // chunks, tt, ss, q], z, tt, ss,
            ).wait_recv()
            return c

        lax.fori_loop(0, span * chunks, rows_in, 0)

    keep_col.wait()
    keep_panel.wait()
    keep_squares.wait()

    def finish(i, c):
        b, q = i // chunks, lax.rem(i, chunks)
        owner = b // span

        @pl.when(owner == rank)
        def _():
            row_keep(b, q).wait()

        @pl.when(owner != rank)
        def _():
            row_copy(b, q, owner // sub_count, lax.rem(owner, sub_count)).wait_send()

        @pl.when(jnp.logical_and(b <= z, z < z_count - 1))
        def _():
            hop(b, q, 1).wait_send()

        @pl.when(jnp.logical_and(b >= z, z > 0))
        def _():
            hop(b, q, 0).wait_send()

        return c

    lax.fori_loop(0, z_count * chunks, finish, 0)


def gather_tokens(tokens, panel_index, row_count):
    z_count, tok_count, sub_count = (lax.axis_size(a) for a in ("cols", "tok", "sub"))
    depth, width = tokens.shape[0] // sub_count, tokens.shape[1]
    span = row_count // width
    chunks = 4 if z_count <= 4 else 1
    dma = pltpu.SemaphoreType.DMA
    team = (tok_count, sub_count)
    anywhere = pl.BlockSpec(memory_space=pl.ANY)
    rows, cols, panel, squares = pl.pallas_call(
        gather_kernel,
        out_shape=[
            jax.ShapeDtypeStruct((span, *team, depth, width), jnp.bfloat16),
            jax.ShapeDtypeStruct((*team, depth, width), jnp.bfloat16),
            jax.ShapeDtypeStruct((*team, depth, PANEL), jnp.bfloat16),
            jax.ShapeDtypeStruct((*team, 16, 128), jnp.float32),
        ],
        in_specs=[pl.BlockSpec(memory_space=pltpu.SMEM), anywhere],
        out_specs=[anywhere] * 4,
        scratch_shapes=[
            pltpu.VMEM((z_count, depth, width), jnp.bfloat16),
            pltpu.VMEM((depth, PANEL), jnp.bfloat16),
            pltpu.VMEM((16, 128), jnp.float32),
            dma((2, z_count, chunks)), dma((z_count, chunks)),
            dma((z_count, chunks)), dma((span, *team, chunks)),
            dma(team), dma(team), dma(team), dma(team), dma(team), dma(team),
            dma((4,)), dma((span, chunks)),
        ],
        compiler_params=pltpu.CompilerParams(
            collective_id=0, has_side_effects=True, vmem_limit_bytes=32 << 20
        ),
        name="gather",
    )(panel_index, tokens)
    total = tok_count * tokens.shape[0]
    rows = jnp.swapaxes(rows.reshape(span, total, width), 0, 1).reshape(total, row_count)
    return rows, cols.reshape(total, width), panel.reshape(total, PANEL), jnp.sum(squares)


def body(tokens, damp_ratio, panel_index):
    col_width = tokens.shape[1]
    row_count = D // (lax.axis_size("tok") * lax.axis_size("sub"))
    total = tokens.shape[0] * lax.axis_size("tok")
    scale = 2.0 / total
    row_rank = lax.axis_index(("tok", "sub"))
    col_rank = lax.axis_index("cols")
    row_index = row_rank * row_count + jnp.arange(row_count, dtype=jnp.int32)
    col_index = col_rank * col_width + jnp.arange(col_width, dtype=jnp.int32)

    start = panel_index[0] * PANEL
    end = start + PANEL
    own_rows, own_cols, in_panel, squares = gather_tokens(tokens, panel_index, row_count)
    damping = damp_ratio[0].astype(jnp.float32) / 100.0 * (squares * scale / D)

    square = dot_bf16(in_panel, in_panel, ((0,), (0,))) * scale
    square = square + damping * jnp.eye(PANEL, dtype=jnp.float32)
    factor, inverse = factor_and_inverse(square)

    lead = sum(dot_bf16(part, in_panel, ((1,), (1,))) for part in split_bf16(inverse, 3)) * scale
    lead_high, lead_low = split_bf16(lead, 2)

    def solved(x):
        return dot_bf16(lead_high, x, ((1,), (0,))) + dot_bf16(lead_low, x, ((1,), (0,)))

    rows_solved = solved(own_rows)
    cols_solved = solved(own_cols)
    panel_out = jnp.where(row_index[:, None] >= end, rows_solved.T, 0.0)
    offset = start - row_rank * row_count
    holds = (offset >= 0) & (offset < row_count)
    offset = jnp.clip(offset, 0, row_count - PANEL)
    kept = lax.dynamic_slice_in_dim(panel_out, offset, PANEL, 0)
    panel_out = lax.dynamic_update_slice_in_dim(panel_out, jnp.where(holds, factor, kept), offset, 0)

    row_high, row_low = split_bf16(jnp.where(row_index[None, :] >= end, rows_solved, 0.0), 2)
    col_high, col_low = split_bf16(jnp.where(col_index[None, :] >= end, cols_solved * (-1.0 / scale), 0.0), 2)
    left = jnp.concatenate([own_rows, row_high, row_high, row_low], 0)
    right = jnp.concatenate([own_cols, col_high, col_low, col_high], 0)
    updated = dot_bf16(left, right, ((0,), (0,))) * scale
    updated = updated + jnp.where(row_index[:, None] == col_index[None, :], damping, 0.0)
    return (updated, panel_out)


def solution(mesh):
    placed = (P(("groups", "tok"), "cols"), P("groups"), P("groups"))
    return jax.shard_map(
        body,
        mesh=mesh,
        in_specs=placed,
        out_specs=(P(("groups", "tok", "sub"), "cols"), P(("groups", "tok", "sub"), None)),
        check_vma=False,
    )
```
